32 devices in a mesh: passage: 4 (over z), span: 8 (over y, x, core).
Axes of the slice: x: 2, y: 2, z: 4, core: 2. Of those that a mesh axis runs over, the one named last changes fastest.
Arguments:
- psi_rotor: float32 [6, 64, 64, 128], P(None, 'passage', 'span'), may hold values from -11 to 11
- psi_stator: float32 [6, 64, 64, 128], P(None, 'passage', 'span'), may hold values from -6 to 6
- rhs_rotor: float32 [6, 64, 64, 128], P(None, 'passage', 'span'), may hold values from -6 to 6
- rhs_stator: float32 [6, 64, 64, 128], P(None, 'passage', 'span'), may hold values from -6 to 6
- kappa_rotor: float32 [64, 64, 128], P('passage', 'span'), may hold values from 1 to 4
- kappa_stator: float32 [64, 64, 128], P('passage', 'span'), may hold values from 1 to 4
- rotor_blocks: float32 [7, 6, 6], replicated, may hold values from -0.5 to 1
- stator_blocks: float32 [7, 6, 6], replicated, may hold values from -0.5 to 1
- interface_block: float32 [6, 6], replicated, may hold values from -0.5 to 0.7
- pass_counts: int32 [4], P('passage'), may hold values from 8 to 16
- tile_source: int32 [8], replicated, may hold values from 0 to 7, as said below
Outputs:
- rotor_out: float32 [6, 64, 64, 128], P(None, 'passage', 'span')
- stator_out: float32 [6, 64, 64, 128], P(None, 'passage', 'span')
The draws below stay inside these ranges and needn't reach their ends.
Inputs may be any that keep to these rules, and one draw needn't show every extreme that they name: `tile_source`: each stator span tile names one rotor span tile.
All inputs are finite; a program needn't handle non-finite values.
Results may differ from the reference program's by a relative error of at most 0.00011.
Values sent between devices are 32-bit elements; how exact they have to be, the bound alone decides.
A program may use at most 64 MiB of HBM per device.

```python
import math
import jax
import jax.numpy as jnp
from jax import lax

F = 6
CP = 16
CS = 8
CA = 128
ITERS = 3
PITCH = 64
SPANS = 64
NBLOCKS = 4
NTILES = 8


def draw_psi_rotor(key, part):
    first, second = jax.random.split(key)
    base = jnp.clip(jax.random.normal(first, (F, 1, SPANS, CA), jnp.float32), -4.0, 4.0)
    position = (jnp.arange(PITCH) % CP).astype(jnp.float32) / CP
    wake = (0.4 + 1.6 * position).reshape(1, PITCH, 1, 1)
    noise = 0.7 * jnp.clip(jax.random.normal(second, (F, PITCH, SPANS, CA), jnp.float32), -3.0, 3.0)
    return base * wake + noise


def make_blocks(key):
    eye = jnp.eye(F, dtype=jnp.float32)
    center_noise = jnp.clip(jax.random.normal(jax.random.fold_in(key, 11), (F, F), jnp.float32), -3.0, 3.0)
    center = eye + 0.12 * center_noise * (1.0 - eye)
    side_noise = jnp.clip(jax.random.normal(jax.random.fold_in(key, 12), (6, F, F), jnp.float32), -3.0, 3.0)
    sides = 0.08 * eye[None] + 0.05 * side_noise
    return jnp.concatenate([center[None], sides], axis=0)


def draw_rotor_blocks(key, part):
    return make_blocks(jax.random.fold_in(key, 21))


def draw_stator_blocks(key, part):
    return make_blocks(jax.random.fold_in(key, 22))


def draw_interface_block(key, part):
    eye = jnp.eye(F, dtype=jnp.float32)
    noise = jnp.clip(jax.random.normal(jax.random.fold_in(key, 31), (F, F), jnp.float32), -3.0, 3.0)
    return 0.6 * eye + 0.15 * noise * (1.0 - eye)


def draw_pass_counts(key, part):
    lowest = max(1, CP // 2)
    counts = jax.random.randint(jax.random.fold_in(key, 41), (NBLOCKS,), lowest, CP + 1)
    where = jax.random.randint(jax.random.fold_in(key, 42), (), 0, NBLOCKS)
    counts = counts.at[where].set(CP)
    counts = counts.at[(where + 1) % NBLOCKS].set(lowest)
    return counts.astype(jnp.int32)


def draw_tile_source(key, part):
    source = jax.random.randint(jax.random.fold_in(key, 51), (NTILES,), 0, NTILES)
    where = jax.random.randint(jax.random.fold_in(key, 52), (), 0, NTILES)
    source = source.at[where].set((where + NTILES // 2) % NTILES)
    source = source.at[(where + 1) % NTILES].set(0)
    source = source.at[(where + 2) % NTILES].set(NTILES - 1)
    return source.astype(jnp.int32)


def block_levels(rng, extent, cuts, least, top_value):
    level, own = 1.0, jax.random.fold_in(rng, 6)
    for dim, blocks in cuts:
        heights = jnp.exp(jax.random.uniform(jax.random.fold_in(own, dim), (blocks,), jnp.float32, least / len(cuts), top_value / len(cuts)))
        level = level * jnp.repeat(heights, extent[dim] // blocks).reshape([-1 if axis == dim else 1 for axis in range(len(extent))])
    return level


def normal_values(stream_key, extent, deviation, most, pieces=(), kind=jnp.bfloat16):
    loudness = block_levels(stream_key, extent, pieces, -0.22, 0.18) if pieces else 1.0
    entries = jax.random.normal(stream_key, extent, jnp.float32) * deviation * loudness
    return jnp.minimum(jnp.maximum(entries, -most), most).astype(kind)


def setup_inputs(seed: int = 0) -> dict:
    splits = jax.random.split(jax.random.key(seed), 12)
    return {
        "psi_rotor": draw_psi_rotor(jax.random.fold_in(splits[11], 71), 0),
        "psi_stator": normal_values(splits[1], (F, PITCH, SPANS, CA), 1.0, 6.0, ((1, 4), (2, 8)), jnp.float32),
        "rhs_rotor": normal_values(splits[2], (F, PITCH, SPANS, CA), 1.0, 6.0, ((1, 4), (2, 8)), jnp.float32),
        "rhs_stator": normal_values(splits[3], (F, PITCH, SPANS, CA), 1.0, 6.0, ((1, 4), (2, 8)), jnp.float32),
        "kappa_rotor": jnp.clip(jnp.exp(math.log(4.0) - 1.3862944 * jax.random.uniform(splits[4], (PITCH, SPANS, CA), jnp.float32) ** block_levels(splits[4], (PITCH, SPANS, CA), ((0, 4), (1, 8)), -0.2, 0.2)), 1.0, 4.0),
        "kappa_stator": jnp.clip(jnp.exp(math.log(4.0) - 1.3862944 * jax.random.uniform(splits[5], (PITCH, SPANS, CA), jnp.float32) ** block_levels(splits[5], (PITCH, SPANS, CA), ((0, 4), (1, 8)), -0.2, 0.2)), 1.0, 4.0),
        "rotor_blocks": draw_rotor_blocks(jax.random.fold_in(splits[11], 71), 0),
        "stator_blocks": draw_stator_blocks(jax.random.fold_in(splits[11], 71), 0),
        "interface_block": draw_interface_block(jax.random.fold_in(splits[11], 71), 0),
        "pass_counts": draw_pass_counts(jax.random.fold_in(splits[11], 71), 0),
        "tile_source": draw_tile_source(jax.random.fold_in(splits[11], 71), 0),
    }


def apply_block(block, field):
    return jnp.einsum("fg,gpsa->fpsa", block, field, precision=lax.Precision.HIGHEST)


def operator(field, kappa, blocks):
    pad_span = jnp.pad(field, ((0, 0), (0, 0), (1, 1), (0, 0)))
    pad_axial = jnp.pad(field, ((0, 0), (0, 0), (0, 0), (1, 1)))
    total = apply_block(blocks[1], jnp.roll(field, 1, axis=1))
    total = total + apply_block(blocks[2], jnp.roll(field, -1, axis=1))
    total = total + apply_block(blocks[3], pad_span[:, :, :-2])
    total = total + apply_block(blocks[4], pad_span[:, :, 2:])
    total = total + apply_block(blocks[5], pad_axial[:, :, :, :-2])
    total = total + apply_block(blocks[6], pad_axial[:, :, :, 2:])
    return kappa[None] * apply_block(blocks[0], field) - total


def reference(psi_rotor, psi_stator, rhs_rotor, rhs_stator, kappa_rotor, kappa_stator, rotor_blocks, stator_blocks, interface_block, pass_counts, tile_source):
    pitch_index = jnp.arange(PITCH, dtype=jnp.int32)
    mask = (pitch_index % CP < pass_counts[pitch_index // CP]).astype(jnp.float32)
    for step in range(ITERS):
        face = psi_rotor[:, :, :, CA - 1] * mask[None, :, None]
        face_mean = jnp.sum(face, axis=1) / jnp.sum(mask)
        inflow = face_mean.reshape(F, NTILES, CS)[:, tile_source].reshape(F, SPANS)
        inlet = jnp.dot(interface_block, inflow, precision=lax.Precision.HIGHEST)
        res_rotor = rhs_rotor - operator(psi_rotor, kappa_rotor, rotor_blocks)
        res_stator = rhs_stator - operator(psi_stator, kappa_stator, stator_blocks)
        res_stator = res_stator.at[:, :, :, 0].add(inlet[:, None, :])
        psi_rotor = psi_rotor + 0.8 * res_rotor / kappa_rotor[None]
        psi_stator = psi_stator + 0.8 * res_stator / kappa_stator[None]
    return psi_rotor, psi_stator
```

```python
import functools

import jax
import jax.numpy as jnp
from jax import lax
from jax.experimental import pallas as pl
from jax.experimental.pallas import tpu as pltpu
from jax.sharding import PartitionSpec as P

ITERS = 3
RELAX = 0.8
MESH = pl.DeviceIdType.MESH
F32 = jnp.float32
BF16 = jnp.bfloat16
ROTOR, STATOR = 0, 1


def split(x):
    hi = x.astype(BF16)
    lo = (x - hi.astype(F32)).astype(BF16)
    return hi, lo


def kernel(fields, cp, cs, ca, npass, nspan, *refs):
    it = iter(refs)

    def take(n):
        return [next(it) for _ in range(n)]

    psi_in = take(2)
    rhs_in = take(2)
    kap_in = take(2)
    blocks = take(2)
    (iface, counts, source) = take(3)
    outs = take(2)
    psi = [take(ITERS + 1) for _ in range(2)]
    rhs = take(2)
    coef = take(2)
    cen = [[take(2) for _ in range(ITERS)] for _ in range(2)]
    ext = [[take(2) for _ in range(ITERS)] for _ in range(2)]
    mat = take(2)
    (psend, precv, ssend, srecv, fsend, frecv, msend) = take(7)
    mrecv = take(ITERS)
    (in_sem, out_sem, hs_sem, hr_sem, fs_sem, fr_sem, ms_sem, mr_sem) = take(8)

    nb = fields * cs
    kx = 2 * nb + 16
    plane = cp * cs

    ip = lax.axis_index("passage")
    js = lax.axis_index("span")
    right = lax.rem(ip + 1, npass)
    left = lax.rem(ip + npass - 1, npass)

    loads = {}
    for n, (src, dst, name) in enumerate(
        [
            (psi_in[0], psi[0][0], "psi0"),
            (psi_in[1], psi[1][0], "psi1"),
            (kap_in[0], coef[0], "kap0"),
            (rhs_in[0], rhs[0], "rhs0"),
            (kap_in[1], coef[1], "kap1"),
            (rhs_in[1], rhs[1], "rhs1"),
        ]
    ):
        loads[name] = pltpu.make_async_copy(src, dst, in_sem.at[n])
        loads[name].start()

    srecv[...] = jnp.zeros_like(srecv)

    barrier = pltpu.get_barrier_semaphore()
    for o in range(1, npass):
        pl.semaphore_signal(
            barrier, inc=1, device_id=(lax.rem(ip + o, npass), js), device_id_type=MESH
        )
    for o in range(1, nspan):
        pl.semaphore_signal(
            barrier, inc=1, device_id=(ip, lax.rem(js + o, nspan)), device_id_type=MESH
        )

    def halo_copies(r, k):
        made = []
        for d, target in ((0, (right, js)), (1, (left, js))):
            made.append(
                pltpu.make_async_remote_copy(
                    src_ref=psend.at[r, k, d],
                    dst_ref=precv.at[r, k, d],
                    send_sem=hs_sem.at[r, k, d],
                    recv_sem=hr_sem.at[r, k, d],
                    device_id=target,
                    device_id_type=MESH,
                )
            )
        for d, target in (
            (0, (ip, lax.rem(js + 1, nspan))),
            (1, (ip, lax.rem(js + nspan - 1, nspan))),
        ):
            made.append(
                pltpu.make_async_remote_copy(
                    src_ref=ssend.at[r, k, d],
                    dst_ref=srecv.at[r, k, d, pl.ds(0, fields * cp)],
                    send_sem=hs_sem.at[r, k, 2 + d],
                    recv_sem=hr_sem.at[r, k, 2 + d],
                    device_id=target,
                    device_id_type=MESH,
                )
            )
        return made

    halos = {(r, k): halo_copies(r, k) for r in range(2) for k in range(ITERS)}
    has_next, has_prev = js < nspan - 1, js > 0

    def send_halos(r, k):
        for d, p in ((0, cp - 1), (1, 0)):
            for f in range(fields):
                psend[r, k, d, pl.ds(f * cs, cs), :] = psi[r][k][
                    pl.ds(f * plane + p * cs, cs), :
                ]
        for d, s in ((0, cs - 1), (1, 0)):
            for f in range(fields):
                ssend[r, k, d, pl.ds(f * cp, cp), :] = psi[r][k][
                    pl.ds(f * plane + s, cp, stride=cs), :
                ]
        to_right, to_left, to_next, to_prev = halos[r, k]

        @pl.when(has_next)
        def _():
            to_next.start()

        @pl.when(has_prev)
        def _():
            to_prev.start()

        to_right.start()
        to_left.start()

    def finish_sends(r, k):
        to_right, to_left, to_next, to_prev = halos[r, k]
        to_right.wait_send()
        to_left.wait_send()

        @pl.when(has_next)
        def _():
            to_next.wait_send()

        @pl.when(has_prev)
        def _():
            to_prev.wait_send()

    def receive_halos(r, k):
        to_right, to_left, to_next, to_prev = halos[r, k]
        to_right.wait_recv()
        to_left.wait_recv()

        @pl.when(has_prev)
        def _():
            to_next.wait_recv()

        @pl.when(has_next)
        def _():
            to_prev.wait_recv()

        chi, clo = cen[r][k]
        for d, p in ((0, 0), (1, cp + 1)):
            hi, lo = split(precv[r, k, d])
            chi[pl.ds(p * nb, nb), :] = hi
            clo[pl.ds(p * nb, nb), :] = lo
        xhi, xlo = ext[r][k]
        for p in range(cp):
            rows = [srecv[r, k, d, pl.ds(p, 8, stride=cp), :] for d in range(2)]
            hi, lo = split(jnp.concatenate(rows, axis=0))
            xhi[pl.ds(p * kx + 2 * nb, 16), :] = hi
            xlo[pl.ds(p * kx + 2 * nb, 16), :] = lo

    lane = lax.broadcasted_iota(jnp.int32, (cs, ca), 1)
    wide = lax.broadcasted_iota(jnp.int32, (nb, ca), 1)

    def face_copies(k):
        return [
            pltpu.make_async_remote_copy(
                src_ref=fsend.at[k],
                dst_ref=frecv.at[k, o],
                send_sem=fs_sem.at[k, o],
                recv_sem=fr_sem.at[k, o],
                device_id=(lax.rem(ip + o, npass), js),
                device_id_type=MESH,
            )
            for o in range(1, npass)
        ]

    def mean_copies(k):
        return [
            pltpu.make_async_remote_copy(
                src_ref=msend.at[k],
                dst_ref=mrecv[k].at[js],
                send_sem=ms_sem.at[k, o],
                recv_sem=mr_sem.at[k, o],
                device_id=(ip, lax.rem(js + o, nspan)),
                device_id_type=MESH,
            )
            for o in range(1, nspan)
        ]

    faces = [face_copies(k) for k in range(ITERS)]
    means = [mean_copies(k) for k in range(ITERS)]
    count = counts[0]

    def send_face(k):
        state = psi[ROTOR][k]
        tile = jnp.where(lane == fields, jnp.clip(count, 0, cp).astype(F32), 0.0)
        for f in range(fields):
            acc = jnp.zeros((cs, ca), F32)
            for p in range(cp):
                w = jnp.where(p < count, 1.0, 0.0).astype(F32)
                acc = acc + w * state[pl.ds(f * plane + p * cs, cs), :]
            tile = jnp.where(lane == f, pltpu.roll(acc, f + 1, 1), tile)
        fsend[k] = tile
        for c in faces[k]:
            c.start()

    def send_mean(k):
        total = fsend[k]
        for o, c in enumerate(faces[k]):
            c.wait_recv()
            total = total + frecv[k, o + 1]
        mean = total / total[:, fields : fields + 1]
        msend[k] = mean
        mrecv[k][js] = mean
        for c in means[k]:
            c.start()

    def inlet_rows(k):
        for c in means[k]:
            c.wait_recv()
        tile = mrecv[k][source[js]]
        moved = [
            jnp.where(lane == 0, pltpu.roll(tile, (ca - g) % ca, 1), 0.0) for g in range(fields)
        ]
        rows = []
        for f in range(fields):
            acc = iface[f, 0] * moved[0]
            for g in range(1, fields):
                acc = acc + iface[f, g] * moved[g]
            rows.append(acc)
        return jnp.concatenate(rows, axis=0)

    def build_matrix(r):
        kk = 5 * nb + 16
        col = lax.broadcasted_iota(jnp.int32, (cs, kk), 1)
        row = lax.broadcasted_iota(jnp.int32, (cs, kk), 0)
        part = col // nb
        g_in = (col - part * nb) // cs
        s_in = col - part * nb - g_in * cs
        tail = part == 5
        up = tail & (g_in == 0)
        down = tail & (g_in == 1)
        which = jnp.full((cs, kk), -1, jnp.int32)
        same = s_in == row
        which = jnp.where((part == 0) & same, 1, which)
        which = jnp.where((part == 2) & same, 2, which)
        which = jnp.where((part == 3) & same, 5, which)
        which = jnp.where((part == 4) & same, 6, which)
        which = jnp.where((part == 1) & (s_in + 1 == row), 3, which)
        which = jnp.where((part == 1) & (s_in == row + 1), 4, which)
        which = jnp.where(up & (row == 0), 3, which)
        which = jnp.where(down & (row == cs - 1), 4, which)
        field = jnp.where(tail, s_in, g_in)
        code = jnp.where(which >= 0, which * 8 + field, -1)
        middle = jnp.where((part == 1) & same, g_in, -1)
        near, main = [], []
        masks = [[code == (b * 8 + g) for g in range(fields)] for b in range(1, 7)]
        centre = [middle == g for g in range(fields)]
        for f in range(fields):
            acc = jnp.zeros((cs, kk), F32)
            mid = jnp.zeros((cs, kk), F32)
            for g in range(fields):
                mid = jnp.where(centre[g], -RELAX * blocks[r][0, f, g], mid)
                for b in range(1, 7):
                    acc = jnp.where(masks[b - 1][g], blocks[r][b, f, g], acc)
            near.append(acc)
            main.append(mid)
        hi, lo = split(jnp.concatenate(near + main, axis=0))
        mat[r][pl.ds(0, 2 * nb), :] = hi
        mat[r][pl.ds(2 * nb, 2 * nb), :] = lo

    def store_split(r, k, p, new):
        chi, clo = cen[r][k]
        xhi, xlo = ext[r][k]
        hi, lo = split(new)
        at = pl.ds(pl.multiple_of((p + 1) * nb, 16), nb)
        chi[at, :] = hi
        clo[at, :] = lo
        before = jnp.where(wide == 0, 0.0, pltpu.roll(new, 1, 1))
        after = jnp.where(wide == ca - 1, 0.0, pltpu.roll(new, ca - 1, 1))
        for n, value in enumerate((before, after)):
            hi, lo = split(value)
            at = pl.ds(pl.multiple_of(p * kx + n * nb, 16), nb)
            xhi[at, :] = hi
            xlo[at, :] = lo

    def cell(ref, p):
        return jnp.concatenate(
            [ref[pl.ds(pl.multiple_of(f * plane + p * cs, 8), cs), :] for f in range(fields)],
            axis=0,
        )

    def columns(c, x, p):
        return jnp.concatenate(
            [
                c[pl.ds(pl.multiple_of(p * nb, 16), 3 * nb), :],
                x[pl.ds(pl.multiple_of(p * kx, 16), kx), :],
            ],
            axis=0,
        )

    def advance(r, k, inlet):
        chi, clo = cen[r][k]
        xhi, xlo = ext[r][k]

        def pair(q):
            cells = (2 * q, 2 * q + 1)
            hi = jnp.concatenate([columns(chi, xhi, p) for p in cells], axis=1)
            lo = jnp.concatenate([columns(clo, xlo, p) for p in cells], axis=1)
            first = jnp.dot(mat[r][...], hi, preferred_element_type=F32)
            second = jnp.dot(mat[r][pl.ds(0, 2 * nb), :], lo, preferred_element_type=F32)
            both = first[: 2 * nb] + (first[2 * nb :] + second)
            for n, p in enumerate(cells):
                mine = both[:, n * ca : (n + 1) * ca]
                res = cell(rhs[r], p) + mine[:nb]
                if inlet is not None:
                    res = res + inlet
                c = coef[r][pl.ds(pl.multiple_of(p * cs, 8), cs), :]
                c = jnp.concatenate([c] * fields, axis=0)
                new = (cell(psi[r][k], p) + mine[nb:]) + c * res
                for f in range(fields):
                    psi[r][k + 1][pl.ds(pl.multiple_of(f * plane + p * cs, 8), cs), :] = new[
                        f * cs : (f + 1) * cs
                    ]
                if k + 1 < ITERS:
                    store_split(r, k + 1, p, new)

        pl.loop(0, cp // 2)(pair)

    pl.semaphore_wait(barrier, npass + nspan - 2)
    loads["psi0"].wait()
    send_halos(ROTOR, 0)
    send_face(0)
    loads["psi1"].wait()
    send_halos(STATOR, 0)

    for r in range(2):
        build_matrix(r)
        pl.loop(0, cp)(lambda p, r=r: store_split(r, 0, p, cell(psi[r][0], p)))
    for r in range(2):
        loads["kap%d" % r].wait()
        coef[r][...] = RELAX / coef[r][...]
        loads["rhs%d" % r].wait()

    stores = []
    for k in range(ITERS):
        send_mean(k)
        receive_halos(ROTOR, k)
        advance(ROTOR, k, None)
        if k + 1 < ITERS:
            send_halos(ROTOR, k + 1)
            send_face(k + 1)
        else:
            stores.append(pltpu.make_async_copy(psi[ROTOR][ITERS], outs[ROTOR], out_sem.at[0]))
            stores[-1].start()
        inlet = inlet_rows(k)
        receive_halos(STATOR, k)
        advance(STATOR, k, inlet)
        if k + 1 < ITERS:
            send_halos(STATOR, k + 1)
    stores.append(pltpu.make_async_copy(psi[STATOR][ITERS], outs[STATOR], out_sem.at[1]))
    stores[-1].start()
    for k in range(ITERS):
        for r in range(2):
            finish_sends(r, k)
        for c in faces[k] + means[k]:
            c.wait_send()
    for c in stores:
        c.wait()


def per_device(
    npass,
    nspan,
    psi_rotor,
    psi_stator,
    rhs_rotor,
    rhs_stator,
    kappa_rotor,
    kappa_stator,
    rotor_blocks,
    stator_blocks,
    interface_block,
    pass_counts,
    tile_source,
):
    fields, cp, cs, ca = psi_rotor.shape
    rows = fields * cp * cs
    flat = [x.reshape(rows, ca) for x in (psi_rotor, psi_stator, rhs_rotor, rhs_stator)]
    kaps = [x.reshape(cp * cs, ca) for x in (kappa_rotor, kappa_stator)]
    nb = fields * cs
    kx = 2 * nb + 16
    state = pltpu.VMEM((rows, ca), F32)
    scratch = [state] * (2 * (ITERS + 1))
    scratch += [state] * 2
    scratch += [pltpu.VMEM((cp * cs, ca), F32)] * 2
    scratch += [pltpu.VMEM(((cp + 2) * nb, ca), BF16)] * (2 * ITERS * 2)
    scratch += [pltpu.VMEM((cp * kx, ca), BF16)] * (2 * ITERS * 2)
    scratch += [pltpu.VMEM((4 * nb, 5 * nb + 16), BF16)] * 2
    scratch += [
        pltpu.VMEM((2, ITERS, 2, nb, ca), F32),
        pltpu.VMEM((2, ITERS, 2, nb, ca), F32),
        pltpu.VMEM((2, ITERS, 2, fields * cp, ca), F32),
        pltpu.VMEM((2, ITERS, 2, 8 * cp, ca), F32),
        pltpu.VMEM((ITERS, cs, ca), F32),
        pltpu.VMEM((ITERS, npass, cs, ca), F32),
        pltpu.VMEM((ITERS, cs, ca), F32),
    ]
    scratch += [pltpu.VMEM((nspan, cs, ca), F32)] * ITERS
    dma = pltpu.SemaphoreType.DMA
    scratch += [
        dma((6,)),
        dma((2,)),
        dma((2, ITERS, 4)),
        dma((2, ITERS, 4)),
        dma((ITERS, npass)),
        dma((ITERS, npass)),
        dma((ITERS, nspan)),
        dma((ITERS, nspan)),
    ]
    anywhere = pl.BlockSpec(memory_space=pltpu.HBM)
    smem = pl.BlockSpec(memory_space=pltpu.SMEM)
    out = pl.pallas_call(
        functools.partial(kernel, fields, cp, cs, ca, npass, nspan),
        out_shape=[jax.ShapeDtypeStruct((rows, ca), F32)] * 2,
        in_specs=[anywhere] * 6 + [smem] * 5,
        out_specs=[anywhere] * 2,
        scratch_shapes=scratch,
        compiler_params=pltpu.CompilerParams(
            collective_id=0, has_side_effects=True, vmem_limit_bytes=40 * 1024 * 1024
        ),
    )(*flat, *kaps, rotor_blocks, stator_blocks, interface_block, pass_counts, tile_source)
    return tuple(x.reshape(psi_rotor.shape) for x in out)


def solution(mesh):
    return jax.shard_map(
        functools.partial(per_device, mesh.shape["passage"], mesh.shape["span"]),
        mesh=mesh,
        in_specs=(
            P(None, "passage", "span", None),
            P(None, "passage", "span", None),
            P(None, "passage", "span", None),
            P(None, "passage", "span", None),
            P("passage", "span", None),
            P("passage", "span", None),
            P(),
            P(),
            P(),
            P("passage"),
            P(),
        ),
        out_specs=(P(None, "passage", "span", None), P(None, "passage", "span", None)),
        check_vma=False,
    )
```

```python
import functools

import jax
import jax.numpy as jnp
from jax import lax
from jax.experimental import pallas as pl
from jax.experimental.pallas import tpu as pltpu
from jax.sharding import PartitionSpec as P

ITERS = 3
RELAX = 0.8
MESH = pl.DeviceIdType.MESH
F32 = jnp.float32
BF16 = jnp.bfloat16
ROTOR, STATOR = 0, 1


def split(x):
    hi = x.astype(BF16)
    lo = (x - hi.astype(F32)).astype(BF16)
    return hi, lo


def kernel(fields, cp, cs, ca, npass, nspan, *refs):
    it = iter(refs)

    def take(n):
        return [next(it) for _ in range(n)]

    psi_in = take(2)
    rhs_in = take(2)
    kap_in = take(2)
    blocks = take(2)
    (iface, counts, source) = take(3)
    outs = take(2)
    psi = [take(ITERS + 1) for _ in range(2)]
    rhs = take(2)
    coef = take(2)
    cen = [[take(2) for _ in range(ITERS)] for _ in range(2)]
    ext = [[take(2) for _ in range(ITERS)] for _ in range(2)]
    mat = take(2)
    (psend, precv, ssend, srecv, fsend, frecv, msend) = take(7)
    mrecv = take(ITERS)
    (in_sem, out_sem, hs_sem, hr_sem, fs_sem, fr_sem, ms_sem, mr_sem) = take(8)

    nb = fields * cs
    kx = 2 * nb + 16
    plane = cp * cs

    ip = lax.axis_index("passage")
    js = lax.axis_index("span")
    right = lax.rem(ip + 1, npass)
    left = lax.rem(ip + npass - 1, npass)

    srecv[...] = jnp.zeros_like(srecv)

    barrier = pltpu.get_barrier_semaphore()
    for o in range(1, npass):
        pl.semaphore_signal(
            barrier, inc=1, device_id=(lax.rem(ip + o, npass), js), device_id_type=MESH
        )
    for o in range(1, nspan):
        pl.semaphore_signal(
            barrier, inc=1, device_id=(ip, lax.rem(js + o, nspan)), device_id_type=MESH
        )

    loads = {}
    for n, (src, dst, name) in enumerate(
        [
            (psi_in[0], psi[0][0], "psi0"),
            (psi_in[1], psi[1][0], "psi1"),
            (kap_in[0], coef[0], "kap0"),
            (rhs_in[0], rhs[0], "rhs0"),
            (kap_in[1], coef[1], "kap1"),
            (rhs_in[1], rhs[1], "rhs1"),
        ]
    ):
        loads[name] = pltpu.make_async_copy(src, dst, in_sem.at[n])
        loads[name].start()

    def halo_copies(r, k):
        made = []
        for d, target in ((0, (right, js)), (1, (left, js))):
            made.append(
                pltpu.make_async_remote_copy(
                    src_ref=psend.at[r, k, d],
                    dst_ref=precv.at[r, k, d],
                    send_sem=hs_sem.at[r, k, d],
                    recv_sem=hr_sem.at[r, k, d],
                    device_id=target,
                    device_id_type=MESH,
                )
            )
        for d, target in (
            (0, (ip, lax.rem(js + 1, nspan))),
            (1, (ip, lax.rem(js + nspan - 1, nspan))),
        ):
            made.append(
                pltpu.make_async_remote_copy(
                    src_ref=ssend.at[r, k, d],
                    dst_ref=srecv.at[r, k, d, pl.ds(0, fields * cp)],
                    send_sem=hs_sem.at[r, k, 2 + d],
                    recv_sem=hr_sem.at[r, k, 2 + d],
                    device_id=target,
                    device_id_type=MESH,
                )
            )
        return made

    halos = {(r, k): halo_copies(r, k) for r in range(2) for k in range(ITERS)}
    has_next, has_prev = js < nspan - 1, js > 0

    def pack_halos(r, k):
        for d, p in ((0, cp - 1), (1, 0)):
            for f in range(fields):
                psend[r, k, d, pl.ds(f * cs, cs), :] = psi[r][k][
                    pl.ds(f * plane + p * cs, cs), :
                ]
        for d, s in ((0, cs - 1), (1, 0)):
            for f in range(fields):
                ssend[r, k, d, pl.ds(f * cp, cp), :] = psi[r][k][
                    pl.ds(f * plane + s, cp, stride=cs), :
                ]

    def start_halos(r, k):
        to_right, to_left, to_next, to_prev = halos[r, k]

        @pl.when(has_next)
        def _():
            to_next.start()

        @pl.when(has_prev)
        def _():
            to_prev.start()

        to_right.start()
        to_left.start()

    def finish_sends(r, k):
        to_right, to_left, to_next, to_prev = halos[r, k]
        to_right.wait_send()
        to_left.wait_send()

        @pl.when(has_next)
        def _():
            to_next.wait_send()

        @pl.when(has_prev)
        def _():
            to_prev.wait_send()

    def receive_halos(r, k):
        to_right, to_left, to_next, to_prev = halos[r, k]
        to_right.wait_recv()
        to_left.wait_recv()

        @pl.when(has_prev)
        def _():
            to_next.wait_recv()

        @pl.when(has_next)
        def _():
            to_prev.wait_recv()

        chi, clo = cen[r][k]
        for d, p in ((0, 0), (1, cp + 1)):
            hi, lo = split(precv[r, k, d])
            chi[pl.ds(p * nb, nb), :] = hi
            clo[pl.ds(p * nb, nb), :] = lo
        xhi, xlo = ext[r][k]
        for p in range(cp):
            rows = [srecv[r, k, d, pl.ds(p, 8, stride=cp), :] for d in range(2)]
            hi, lo = split(jnp.concatenate(rows, axis=0))
            xhi[pl.ds(p * kx + 2 * nb, 16), :] = hi
            xlo[pl.ds(p * kx + 2 * nb, 16), :] = lo

    lane = lax.broadcasted_iota(jnp.int32, (cs, ca), 1)
    wide = lax.broadcasted_iota(jnp.int32, (nb, ca), 1)

    def face_copies(k):
        return [
            pltpu.make_async_remote_copy(
                src_ref=fsend.at[k],
                dst_ref=frecv.at[k, o],
                send_sem=fs_sem.at[k, o],
                recv_sem=fr_sem.at[k, o],
                device_id=(lax.rem(ip + o, npass), js),
                device_id_type=MESH,
            )
            for o in range(1, npass)
        ]

    def mean_copies(k):
        return [
            pltpu.make_async_remote_copy(
                src_ref=msend.at[k],
                dst_ref=mrecv[k].at[js],
                send_sem=ms_sem.at[k, o],
                recv_sem=mr_sem.at[k, o],
                device_id=(ip, lax.rem(js + o, nspan)),
                device_id_type=MESH,
            )
            for o in range(1, nspan)
        ]

    faces = [face_copies(k) for k in range(ITERS)]
    means = [mean_copies(k) for k in range(ITERS)]
    count = counts[0]

    def pack_face(k):
        state = psi[ROTOR][k]
        tile = jnp.where(lane == fields, jnp.clip(count, 0, cp).astype(F32), 0.0)
        for f in range(fields):
            acc = jnp.zeros((cs, ca), F32)
            for p in range(cp):
                w = jnp.where(p < count, 1.0, 0.0).astype(F32)
                acc = acc + w * state[pl.ds(f * plane + p * cs, cs), :]
            tile = jnp.where(lane == f, pltpu.roll(acc, f + 1, 1), tile)
        fsend[k] = tile

    def start_face(k):
        for c in faces[k]:
            c.start()

    def send_mean(k):
        total = fsend[k]
        for o, c in enumerate(faces[k]):
            c.wait_recv()
            total = total + frecv[k, o + 1]
        mean = total / total[:, fields : fields + 1]
        msend[k] = mean
        mrecv[k][js] = mean
        for c in means[k]:
            c.start()

    def inlet_rows(k):
        for c in means[k]:
            c.wait_recv()
        tile = mrecv[k][source[js]]
        moved = [
            jnp.where(lane == 0, pltpu.roll(tile, (ca - g) % ca, 1), 0.0) for g in range(fields)
        ]
        rows = []
        for f in range(fields):
            acc = iface[f, 0] * moved[0]
            for g in range(1, fields):
                acc = acc + iface[f, g] * moved[g]
            rows.append(acc)
        return jnp.concatenate(rows, axis=0)

    def build_matrix(r):
        kk = 5 * nb + 16
        col = lax.broadcasted_iota(jnp.int32, (cs, kk), 1)
        row = lax.broadcasted_iota(jnp.int32, (cs, kk), 0)
        part = col // nb
        g_in = (col - part * nb) // cs
        s_in = col - part * nb - g_in * cs
        tail = part == 5
        up = tail & (g_in == 0)
        down = tail & (g_in == 1)
        which = jnp.full((cs, kk), -1, jnp.int32)
        same = s_in == row
        which = jnp.where((part == 0) & same, 1, which)
        which = jnp.where((part == 2) & same, 2, which)
        which = jnp.where((part == 3) & same, 5, which)
        which = jnp.where((part == 4) & same, 6, which)
        which = jnp.where((part == 1) & (s_in + 1 == row), 3, which)
        which = jnp.where((part == 1) & (s_in == row + 1), 4, which)
        which = jnp.where(up & (row == 0), 3, which)
        which = jnp.where(down & (row == cs - 1), 4, which)
        field = jnp.where(tail, s_in, g_in)
        code = jnp.where(which >= 0, which * 8 + field, -1)
        middle = jnp.where((part == 1) & same, g_in, -1)
        near, main = [], []
        masks = [[code == (b * 8 + g) for g in range(fields)] for b in range(1, 7)]
        centre = [middle == g for g in range(fields)]
        for f in range(fields):
            acc = jnp.zeros((cs, kk), F32)
            mid = jnp.zeros((cs, kk), F32)
            for g in range(fields):
                mid = jnp.where(centre[g], -RELAX * blocks[r][f, 0, g], mid)
                for b in range(1, 7):
                    acc = jnp.where(masks[b - 1][g], blocks[r][f, b, g], acc)
            near.append(acc)
            main.append(mid)
        hi, lo = split(jnp.concatenate(near + main, axis=0))
        mat[r][pl.ds(0, 2 * nb), :] = hi
        mat[r][pl.ds(2 * nb, 2 * nb), :] = lo

    def store_split(r, k, p, new):
        chi, clo = cen[r][k]
        xhi, xlo = ext[r][k]
        hi, lo = split(new)
        at = pl.ds(pl.multiple_of((p + 1) * nb, 16), nb)
        chi[at, :] = hi
        clo[at, :] = lo
        before = jnp.where(wide == 0, 0.0, pltpu.roll(new, 1, 1))
        after = jnp.where(wide == ca - 1, 0.0, pltpu.roll(new, ca - 1, 1))
        for n, value in enumerate((before, after)):
            hi, lo = split(value)
            at = pl.ds(pl.multiple_of(p * kx + n * nb, 16), nb)
            xhi[at, :] = hi
            xlo[at, :] = lo

    def cell(ref, p):
        return jnp.concatenate(
            [ref[pl.ds(pl.multiple_of(f * plane + p * cs, 8), cs), :] for f in range(fields)],
            axis=0,
        )

    def columns(c, x, p):
        return jnp.concatenate(
            [
                c[pl.ds(pl.multiple_of(p * nb, 16), 3 * nb), :],
                x[pl.ds(pl.multiple_of(p * kx, 16), kx), :],
            ],
            axis=0,
        )

    def advance(r, k, inlet):
        chi, clo = cen[r][k]
        xhi, xlo = ext[r][k]

        def pair(q):
            cells = (2 * q, 2 * q + 1)
            hi = jnp.concatenate([columns(chi, xhi, p) for p in cells], axis=1)
            lo = jnp.concatenate([columns(clo, xlo, p) for p in cells], axis=1)
            first = jnp.dot(mat[r][...], hi, preferred_element_type=F32)
            second = jnp.dot(mat[r][pl.ds(0, 2 * nb), :], lo, preferred_element_type=F32)
            both = first[: 2 * nb] + (first[2 * nb :] + second)
            for n, p in enumerate(cells):
                mine = both[:, n * ca : (n + 1) * ca]
                res = cell(rhs[r], p) + mine[:nb]
                if inlet is not None:
                    res = res + inlet
                c = coef[r][pl.ds(pl.multiple_of(p * cs, 8), cs), :]
                c = jnp.concatenate([c] * fields, axis=0)
                new = (cell(psi[r][k], p) + mine[nb:]) + c * res
                for f in range(fields):
                    psi[r][k + 1][pl.ds(pl.multiple_of(f * plane + p * cs, 8), cs), :] = new[
                        f * cs : (f + 1) * cs
                    ]
                if k + 1 < ITERS:
                    store_split(r, k + 1, p, new)

        pl.loop(0, cp // 2, unroll=cp // 2)(pair)

    for r in range(2):
        build_matrix(r)
    for r in range(2):
        loads["psi%d" % r].wait()
        pl.loop(0, cp, unroll=cp)(lambda p, r=r: store_split(r, 0, p, cell(psi[r][0], p)))
        pack_halos(r, 0)
    pack_face(0)
    for r in range(2):
        loads["kap%d" % r].wait()
        coef[r][...] = RELAX / coef[r][...]
        loads["rhs%d" % r].wait()

    pl.semaphore_wait(barrier, npass + nspan - 2)
    start_face(0)
    start_halos(ROTOR, 0)
    start_halos(STATOR, 0)

    stores = []
    for k in range(ITERS):
        send_mean(k)
        receive_halos(ROTOR, k)
        advance(ROTOR, k, None)
        if k + 1 < ITERS:
            pack_face(k + 1)
            start_face(k + 1)
            pack_halos(ROTOR, k + 1)
            start_halos(ROTOR, k + 1)
        else:
            stores.append(pltpu.make_async_copy(psi[ROTOR][ITERS], outs[ROTOR], out_sem.at[0]))
            stores[-1].start()
        inlet = inlet_rows(k)
        receive_halos(STATOR, k)
        advance(STATOR, k, inlet)
        if k + 1 < ITERS:
            pack_halos(STATOR, k + 1)
            start_halos(STATOR, k + 1)
    stores.append(pltpu.make_async_copy(psi[STATOR][ITERS], outs[STATOR], out_sem.at[1]))
    stores[-1].start()
    for k in range(ITERS):
        for r in range(2):
            finish_sends(r, k)
        for c in faces[k] + means[k]:
            c.wait_send()
    for c in stores:
        c.wait()


def per_device(
    npass,
    nspan,
    psi_rotor,
    psi_stator,
    rhs_rotor,
    rhs_stator,
    kappa_rotor,
    kappa_stator,
    rotor_blocks,
    stator_blocks,
    interface_block,
    pass_counts,
    tile_source,
):
    fields, cp, cs, ca = psi_rotor.shape
    rows = fields * cp * cs
    flat = [x.reshape(rows, ca) for x in (psi_rotor, psi_stator, rhs_rotor, rhs_stator)]
    kaps = [x.reshape(cp * cs, ca) for x in (kappa_rotor, kappa_stator)]
    nb = fields * cs
    kx = 2 * nb + 16
    state = pltpu.VMEM((rows, ca), F32)
    scratch = [state] * (2 * (ITERS + 1))
    scratch += [state] * 2
    scratch += [pltpu.VMEM((cp * cs, ca), F32)] * 2
    scratch += [pltpu.VMEM(((cp + 2) * nb, ca), BF16)] * (2 * ITERS * 2)
    scratch += [pltpu.VMEM((cp * kx, ca), BF16)] * (2 * ITERS * 2)
    scratch += [pltpu.VMEM((4 * nb, 5 * nb + 16), BF16)] * 2
    scratch += [
        pltpu.VMEM((2, ITERS, 2, nb, ca), F32),
        pltpu.VMEM((2, ITERS, 2, nb, ca), F32),
        pltpu.VMEM((2, ITERS, 2, fields * cp, ca), F32),
        pltpu.VMEM((2, ITERS, 2, 8 * cp, ca), F32),
        pltpu.VMEM((ITERS, cs, ca), F32),
        pltpu.VMEM((ITERS, npass, cs, ca), F32),
        pltpu.VMEM((ITERS, cs, ca), F32),
    ]
    scratch += [pltpu.VMEM((nspan, cs, ca), F32)] * ITERS
    dma = pltpu.SemaphoreType.DMA
    scratch += [
        dma((6,)),
        dma((2,)),
        dma((2, ITERS, 4)),
        dma((2, ITERS, 4)),
        dma((ITERS, npass)),
        dma((ITERS, npass)),
        dma((ITERS, nspan)),
        dma((ITERS, nspan)),
    ]
    anywhere = pl.BlockSpec(memory_space=pltpu.HBM)
    smem = pl.BlockSpec(memory_space=pltpu.SMEM)
    out = pl.pallas_call(
        functools.partial(kernel, fields, cp, cs, ca, npass, nspan),
        out_shape=[pltpu.HBM((rows, ca), F32)] * 2,
        in_specs=[anywhere] * 6 + [smem] * 5,
        out_specs=[anywhere] * 2,
        scratch_shapes=scratch,
        compiler_params=pltpu.CompilerParams(
            collective_id=0, has_side_effects=True, vmem_limit_bytes=40 * 1024 * 1024
        ),
    )(
        *[pltpu.with_memory_space_constraint(x, pltpu.HBM) for x in flat + kaps],
        rotor_blocks.transpose(1, 0, 2),
        stator_blocks.transpose(1, 0, 2),
        interface_block,
        pass_counts,
        tile_source,
    )
    return tuple(x.reshape(psi_rotor.shape) for x in out)


def solution(mesh):
    return jax.shard_map(
        functools.partial(per_device, mesh.shape["passage"], mesh.shape["span"]),
        mesh=mesh,
        in_specs=(
            P(None, "passage", "span", None),
            P(None, "passage", "span", None),
            P(None, "passage", "span", None),
            P(None, "passage", "span", None),
            P("passage", "span", None),
            P("passage", "span", None),
            P(),
            P(),
            P(),
            P("passage"),
            P(),
        ),
        out_specs=(P(None, "passage", "span", None), P(None, "passage", "span", None)),
        check_vma=False,
    )
```
